32 devices in a mesh: var: 16 (over z, x, core), smp: 2 (over y).
Axes of the slice: x: 2, y: 2, z: 4, core: 2. Of those that a mesh axis runs over, the one named last changes fastest.
Arguments:
- genotypes: bfloat16 [1024, 8192], P('smp', 'var'), may hold values from -4 to 4, as said below
- marginal: float32 [8192, 256], P('var', 'smp'), may hold values from -6 to 6
- block_inverse: float32 [32, 256, 256], P('var'), may hold values from -1 to 1, as said below
Outputs:
- weights: float32 [8192, 256], P('var', 'smp')
The draws below stay inside these ranges and needn't reach their ends.
Inputs may be any that keep to these rules, and one draw needn't show every extreme that they name: `genotypes`: each variant's column has mean about 0 and variance about 1 over the samples. `block_inverse`: matrices near the identity divided by 1.5, with independent entrywise jitter; they are not derived from R.
All inputs are finite; a program needn't handle non-finite values.
Results may differ from the reference program's by a relative error of at most 0.0003.
Values may be sent and summed in bfloat16 or wider, within the bound.
A program may use at most 64 MiB of HBM per device.

```python
import jax
import jax.numpy as jnp
from jax import lax

GROUP = 256
SWEEPS = 2
BAND = 512
VARIANTS = 8192
GROUPS = 32
SAMPLES = 1024
TRAITS = 256


def draw_genotypes(key, part):
    full_shape = (SAMPLES, VARIANTS)
    memory_rate = 0.85
    fresh_share = (1.0 - memory_rate * memory_rate) ** 0.5
    innovation = jax.random.truncated_normal(key, -4.0, 4.0, full_shape, jnp.float32)
    blocks = jnp.transpose(innovation.reshape(SAMPLES, GROUPS, GROUP), (1, 0, 2))

    def carry_step(carried, incoming):
        following = memory_rate * carried + fresh_share * incoming
        return (following, following)
    leading = blocks[0]
    final_block, later_blocks = lax.scan(carry_step, leading, blocks[1:])
    mixed_blocks = jnp.concatenate([leading[None], later_blocks], 0)
    mixed = jnp.transpose(mixed_blocks, (1, 0, 2)).reshape(SAMPLES, VARIANTS)
    return jnp.clip(mixed, -4.0, 4.0).astype(jnp.bfloat16)


def draw_block_inverse(key, part):
    block_shape = (GROUPS, GROUP, GROUP)
    jitter = 0.025 * jax.random.truncated_normal(key, -4.0, 4.0, block_shape, jnp.float32)
    identity = jnp.eye(GROUP, dtype=jnp.float32)
    return (identity + jitter) / 1.5


def level_of(key, dims, cuts, least, high):
    gain = 1.0
    for position, blocks in cuts:
        draws = jax.random.uniform(jax.random.fold_in(jax.random.fold_in(key, 6), position), (blocks,), jnp.float32, least / len(cuts), high / len(cuts))
        gain = gain * jnp.repeat(jnp.exp(draws), dims[position] // blocks).reshape((-1,) + (1,) * (len(dims) - 1 - position))
    return gain


def scatter_about(key, dims, width, most, cuts=(), held_as=jnp.bfloat16):
    level = level_of(key, dims, cuts, -0.22, 0.18) if cuts else 1.0
    result = jax.random.normal(key, dims, jnp.float32) * width * level
    return jnp.minimum(jnp.maximum(result, -most), most).astype(held_as)


def setup_inputs(seed: int = 0) -> dict:
    seeds = jax.random.split(jax.random.key(seed), 4)
    genotypes = draw_genotypes(jax.random.fold_in(seeds[3], 71), 0)
    marginal = scatter_about(seeds[1], (VARIANTS, TRAITS), 1.0, 6.0, ((0, 16), (1, 2)), jnp.float32)
    block_inverse = draw_block_inverse(jax.random.fold_in(seeds[3], 71), 0)
    return {"genotypes": genotypes, "marginal": marginal, "block_inverse": block_inverse}


ridge_weight = 0.5


def one_group(padded, group_index):
    start = (group_index * GROUP).astype(jnp.int32)
    own_cols = lax.dynamic_slice_in_dim(padded, start, GROUP, 1)
    partner = lax.dynamic_slice_in_dim(padded, start, 3 * GROUP, 1)
    whole = jnp.dot(own_cols.T, partner, preferred_element_type=jnp.float32)
    stacked = jnp.transpose(whole.reshape(GROUP, 3, GROUP), (1, 0, 2))
    stacked = jnp.stack([stacked[0], stacked[1], jnp.tril(stacked[2])], 0)
    return stacked / SAMPLES


def slab_sweep(linkage, inverse, weights, target, upstream):
    group = inverse.shape[1]
    band = 2 * group
    count = inverse.shape[0]
    rows = weights.shape[0]
    cols = weights.shape[1]
    padded = jnp.concatenate([jnp.zeros((band, cols), jnp.float32), weights, upstream], 0)
    lowered = jnp.concatenate([jnp.zeros((2, 3, group, group), jnp.float32), linkage], 0)
    highest = lax.Precision.HIGHEST

    def advance(group_index, state):
        base = band + group_index * group
        current = lax.dynamic_slice_in_dim(state, base, group, 0)
        remain = lax.dynamic_slice_in_dim(target, group_index * group, group, 0) - ridge_weight * current
        for offset in range(3):
            remain = remain - jnp.dot(linkage[group_index, offset], lax.dynamic_slice_in_dim(state, base + offset * group, group, 0), precision=highest)
        for offset in (1, 2):
            remain = remain - jnp.dot(lowered[group_index + 2 - offset, offset].T, lax.dynamic_slice_in_dim(state, base - offset * group, group, 0), precision=highest)
        updated = current + jnp.dot(inverse[group_index], remain, precision=highest)
        return lax.dynamic_update_slice_in_dim(state, updated, base, 0)

    padded = lax.fori_loop(0, count, advance, padded)
    return padded[band:band + rows]


def reference(genotypes, marginal, block_inverse):
    padded = jnp.concatenate([genotypes, jnp.zeros((genotypes.shape[0], BAND), genotypes.dtype)], 1)
    linkage = lax.map(lambda group_index: one_group(padded, group_index), jnp.arange(GROUPS, dtype=jnp.int32))
    weights = jnp.zeros(marginal.shape, jnp.float32)
    upstream = jnp.zeros((BAND, marginal.shape[1]), jnp.float32)
    for sweep_index in range(SWEEPS):
        weights = slab_sweep(linkage, block_inverse, weights, marginal, upstream)
    return weights
```

```python
import functools

import jax
import jax.numpy as jnp
from jax import lax
from jax.experimental import pallas as pl
from jax.experimental.pallas import tpu as pltpu
from jax.sharding import PartitionSpec as P

RIDGE = 0.5
CHUNKS = 2
MESH = pl.DeviceIdType.MESH
F32 = jnp.float32
BF16 = jnp.bfloat16


def halves(x):
    high = x.astype(BF16)
    low = (x - high.astype(F32)).astype(BF16)
    return high, low


def dot(a, b):
    return jnp.dot(a, b, preferred_element_type=F32)


def gram(a, b):
    return lax.dot_general(a, b, (((0,), (0,)), ((), ())), preferred_element_type=F32)


def wide(a, b):
    return dot(a[0], b[0]) + (dot(a[0], b[1]) + dot(a[1], b[0]))


def pair_dot(a, both):
    n = both.shape[1] // 2
    first = dot(a[0], both)
    return first[:, :n] + (first[:, n:] + dot(a[1], both[:, :n]))


def joined(x):
    return jnp.concatenate(halves(x), 1)


def kernel(
    var_count, smp_count, total,
    g_ref, m_ref, b_ref, w_ref,
    mates, rim, u_high, u_low, c_high, c_low, w1_f32, w1_out, w1_in, y_out, y_in, w2_out, w2_in,
    mate_send, mate_recv, rim_send, rim_recv, chain_send, chain_recv,
):
    s = lax.axis_index("var")
    q = lax.axis_index("smp")
    last = var_count - 1
    grp = b_ref.shape[1]
    samples = g_ref.shape[0]
    part = samples // CHUNKS
    right = {"var": s + 1}
    left = {"var": s - 1}
    a_rows, b_rows = pl.ds(0, grp), pl.ds(grp, grp)

    barrier = pltpu.get_barrier_semaphore()

    @pl.when(s > 0)
    def _():
        pl.semaphore_signal(barrier, inc=1, device_id=left, device_id_type=MESH)

    @pl.when(s < last)
    def _():
        pl.semaphore_signal(barrier, inc=1, device_id=right, device_id_type=MESH)

    for k in range(1, smp_count):
        pl.semaphore_signal(
            barrier, inc=1, device_id={"smp": lax.rem(q + k, smp_count)}, device_id_type=MESH
        )
    inner = jnp.logical_and(s > 0, s < last)

    @pl.when(inner)
    def _():
        pl.semaphore_wait(barrier, smp_count + 1)

    @pl.when(jnp.logical_not(inner))
    def _():
        pl.semaphore_wait(barrier, smp_count)

    def mate_copy(k, c):
        rows = pl.ds(c * part, part)
        return pltpu.make_async_remote_copy(
            src_ref=g_ref.at[rows],
            dst_ref=mates.at[k - 1, rows],
            send_sem=mate_send.at[k - 1, c],
            recv_sem=mate_recv.at[k - 1, c],
            device_id={"smp": lax.rem(q + k, smp_count)},
            device_id_type=MESH,
        )

    def rim_copy(k, c):
        rows = pl.ds(c * part, part)
        return pltpu.make_async_remote_copy(
            src_ref=g_ref.at[rows] if k == 0 else mates.at[k - 1, rows],
            dst_ref=rim.at[k, rows],
            send_sem=rim_send.at[k, c],
            recv_sem=rim_recv.at[k, c],
            device_id=right,
            device_id_type=MESH,
        )

    def chain_copy(index, src, dst, target):
        return pltpu.make_async_remote_copy(
            src_ref=src,
            dst_ref=dst,
            send_sem=chain_send.at[index],
            recv_sem=chain_recv.at[index],
            device_id=target,
            device_id_type=MESH,
        )

    w1_copy = chain_copy(0, w1_out, w1_in, right)
    y_copy = chain_copy(1, y_out, y_in, left)
    w2_copy = chain_copy(2, w2_out, w2_in, right)

    for c in range(CHUNKS):
        for k in range(1, smp_count):
            mate_copy(k, c).start()

    @pl.when(s < last)
    def _():
        for c in range(CHUNKS):
            rim_copy(0, c).start()

    inverse = [halves(b_ref[0]), halves(b_ref[1])]
    for c in range(CHUNKS):
        for k in range(1, smp_count):
            mate_copy(k, c).wait_recv()

            @pl.when(s < last)
            def _():
                rim_copy(k, c).start()

    def own_block(i, j):
        ci, cj = pl.ds(i * grp, grp), pl.ds(j * grp, grp)
        acc = gram(g_ref[:, ci], g_ref[:, cj])
        for k in range(1, smp_count):
            acc = acc + gram(mates[k - 1, :, ci], mates[k - 1, :, cj])
        return acc * (1.0 / total)

    a_aa = halves(own_block(0, 0))
    a_bb = halves(own_block(1, 1))
    lower_f32 = own_block(1, 0)
    a_ba = halves(lower_f32)
    a_ab = halves(lower_f32.T)
    s21_f32 = -wide(inverse[1], halves(wide(a_ba, inverse[0])))
    s21 = halves(s21_f32)
    v_a = wide(inverse[0], halves(m_ref[a_rows]))
    v_b = wide(inverse[1], halves(m_ref[b_rows] - wide(a_ba, halves(v_a))))

    @pl.when(s == 0)
    def _():
        w1_f32[a_rows] = v_a
        w1_f32[b_rows] = v_b
        w1_out[a_rows] = joined(v_a)
        w1_out[b_rows] = joined(v_b)

    @pl.when(s > 0)
    def _():
        for c in range(CHUNKS):
            for k in range(smp_count):
                rim_copy(k, c).wait_recv()

        def cross_block(i, j):
            ci, cj = pl.ds(i * grp, grp), pl.ds(j * grp, grp)
            acc = gram(g_ref[:, ci], rim[0, :, cj])
            for k in range(1, smp_count):
                acc = acc + gram(mates[k - 1, :, ci], rim[k, :, cj])
            return acc * (1.0 / total)

        row = lax.broadcasted_iota(jnp.int32, (grp, grp), 0)
        col = lax.broadcasted_iota(jnp.int32, (grp, grp), 1)
        within = col >= row
        a0 = jnp.where(within, cross_block(0, 0), 0.0)
        a1 = cross_block(0, 1)
        b1 = jnp.where(within, cross_block(1, 1), 0.0)
        for n, block in enumerate((a0, a1, b1)):
            high, low = halves(block.T)
            c_high[n] = high
            c_low[n] = low
        a0, a1, b1 = halves(a0), halves(a1), halves(b1)

        def put(rows, cols, value):
            high, low = halves(-value)
            u_high[rows, cols] = high
            u_low[rows, cols] = low

        put(a_rows, a_rows, wide(inverse[0], a0))
        put(a_rows, b_rows, wide(inverse[0], a1))
        put(b_rows, a_rows, wide(s21, a0))
        put(b_rows, b_rows, wide(s21, a1) + wide(inverse[1], b1))

        w1_copy.wait_recv()
        step = pair_dot((u_high[...], u_low[...]), w1_in[...])
        w1_a = v_a + step[:grp]
        w1_b = v_b + step[grp:]
        w1_f32[a_rows] = w1_a
        w1_f32[b_rows] = w1_b
        w1_out[a_rows] = joined(w1_a)
        w1_out[b_rows] = joined(w1_b)

    @pl.when(s < last)
    def _():
        w1_copy.start()

    @pl.when(s > 0)
    def _():
        own_a, own_b = w1_out[a_rows], w1_out[b_rows]
        y_out[a_rows] = joined(pair_dot((c_high[0], c_low[0]), own_a))
        y_out[b_rows] = joined(
            pair_dot((c_high[1], c_low[1]), own_a) + pair_dot((c_high[2], c_low[2]), own_b)
        )
        y_copy.start()

    w1_a, w1_b = w1_f32[a_rows], w1_f32[b_rows]
    pair_a, pair_b = w1_out[a_rows], w1_out[b_rows]
    r_a = m_ref[a_rows] - RIDGE * w1_a - pair_dot(a_aa, pair_a) - pair_dot(a_ab, pair_b)
    h_a = w1_a + pair_dot(inverse[0], joined(r_a))
    r_b = m_ref[b_rows] - RIDGE * w1_b - pair_dot(a_bb, pair_b) - pair_dot(a_ba, joined(h_a))
    h_b = w1_b + pair_dot(inverse[1], joined(r_b))
    w_ref[a_rows] = h_a
    w_ref[b_rows] = h_b

    @pl.when(s < last)
    def _():
        y_copy.wait_recv()
        y_a, y_b = y_in[a_rows], y_in[b_rows]
        w_ref[a_rows] -= pair_dot(inverse[0], y_a)
        w_ref[b_rows] -= pair_dot(s21, y_a) + pair_dot(inverse[1], y_b)

    @pl.when(s > 0)
    def _():
        w2_copy.wait_recv()
        w_ref[...] += pair_dot((u_high[...], u_low[...]), w2_in[...])

    @pl.when(s < last)
    def _():
        w2_out[...] = joined(w_ref[...])
        w2_copy.start()

    for c in range(CHUNKS):
        for k in range(1, smp_count):
            mate_copy(k, c).wait_send()

    @pl.when(s < last)
    def _():
        for c in range(CHUNKS):
            for k in range(smp_count):
                rim_copy(k, c).wait_send()
        w1_copy.wait_send()
        w2_copy.wait_send()

    @pl.when(s > 0)
    def _():
        y_copy.wait_send()


def solution(mesh):
    var_count, smp_count = mesh.shape["var"], mesh.shape["smp"]

    def per_device(genotypes, marginal, block_inverse):
        samples, variants = genotypes.shape
        traits = marginal.shape[1]
        grp = block_inverse.shape[1]
        pair = (variants, 2 * traits)
        mates = max(1, smp_count - 1)
        dma = pltpu.SemaphoreType.DMA
        return pl.pallas_call(
            functools.partial(kernel, var_count, smp_count, samples * smp_count),
            out_shape=jax.ShapeDtypeStruct(marginal.shape, F32),
            in_specs=[pl.BlockSpec(memory_space=pltpu.VMEM)] * 3,
            out_specs=pl.BlockSpec(memory_space=pltpu.VMEM),
            scratch_shapes=[
                pltpu.VMEM((mates, samples, variants), BF16),
                pltpu.VMEM((smp_count, samples, variants), BF16),
                pltpu.VMEM((variants, variants), BF16),
                pltpu.VMEM((variants, variants), BF16),
                pltpu.VMEM((3, grp, grp), BF16),
                pltpu.VMEM((3, grp, grp), BF16),
                pltpu.VMEM((variants, traits), F32),
                pltpu.VMEM(pair, BF16),
                pltpu.VMEM(pair, BF16),
                pltpu.VMEM(pair, BF16),
                pltpu.VMEM(pair, BF16),
                pltpu.VMEM(pair, BF16),
                pltpu.VMEM(pair, BF16),
                dma((mates, CHUNKS)),
                dma((mates, CHUNKS)),
                dma((smp_count, CHUNKS)),
                dma((smp_count, CHUNKS)),
                dma((3,)),
                dma((3,)),
            ],
            compiler_params=pltpu.CompilerParams(
                collective_id=0, has_side_effects=True, vmem_limit_bytes=48 * 1024 * 1024
            ),
        )(genotypes, marginal, block_inverse)

    return jax.shard_map(
        per_device,
        mesh=mesh,
        in_specs=(P("smp", "var"), P("var", "smp"), P("var", None, None)),
        out_specs=P("var", "smp"),
        check_vma=False,
    )
```

```python
import functools

import jax
import jax.numpy as jnp
from jax import lax
from jax.experimental import pallas as pl
from jax.experimental.pallas import tpu as pltpu
from jax.sharding import PartitionSpec as P

RIDGE = 0.5
CHUNKS = 4
PARTS = 2
MESH = pl.DeviceIdType.MESH
F32 = jnp.float32
BF16 = jnp.bfloat16


def halves(x):
    high = x.astype(BF16)
    low = (x - high.astype(F32)).astype(BF16)
    return high, low


def dot(a, b):
    return jnp.dot(a, b, preferred_element_type=F32)


def gram(a, b):
    return lax.dot_general(a, b, (((0,), (0,)), ((), ())), preferred_element_type=F32)


def wide(a, b):
    return dot(a[0], b[0]) + (dot(a[0], b[1]) + dot(a[1], b[0]))


def pair_dot(a, both):
    n = both.shape[1] // 2
    first = dot(a[0], both)
    return first[:, :n] + (first[:, n:] + dot(a[1], both[:, :n]))


def joined(x):
    return jnp.concatenate(halves(x), 1)


def kernel(
    var_count, smp_count, total,
    g_hbm, m_hbm, b_hbm, w_hbm,
    g_ref, m_ref, b_ref, w_ref,
    mates, rim, cross, u_high, u_low, in_high, in_low, chip_high, chip_low, c_high, c_low,
    v_f32, v_out, v_in, w1_f32, h_f32, w1_out, x1_in, x1_pass, y_out, y_in, h_out, h_in,
    w2_out, x2_in, x2_pass,
    local_sem, mate_send, mate_recv, rim_send, rim_recv, u_send, u_recv, chain_send, chain_recv,
):
    s = lax.axis_index("var")
    q = lax.axis_index("smp")
    last = var_count - 1
    grp = b_ref.shape[1]
    samples = g_ref.shape[0]
    piece = samples // CHUNKS
    wide_part = m_ref.shape[1] // PARTS
    even = lax.rem(s, 2) == 0
    odd = jnp.logical_not(even)
    right, left = {"var": s + 1}, {"var": s - 1}
    next_chip = {"var": s + 2}
    a_rows, b_rows = pl.ds(0, grp), pl.ds(grp, grp)
    both = jnp.logical_and

    locals_ = [
        pltpu.make_async_copy(g_hbm, g_ref, local_sem.at[0]),
        pltpu.make_async_copy(m_hbm, m_ref, local_sem.at[1]),
        pltpu.make_async_copy(b_hbm, b_ref, local_sem.at[2]),
    ]
    for copy in locals_:
        copy.start()

    barrier = pltpu.get_barrier_semaphore()

    def greet(target):
        pl.semaphore_signal(barrier, inc=1, device_id=target, device_id_type=MESH)

    for k in range(1, smp_count):
        greet({"smp": lax.rem(q + k, smp_count)})
    pl.when(s > 0)(lambda: greet(left))
    pl.when(s < last)(lambda: greet(right))
    pl.when(both(odd, s > 1))(lambda: greet({"var": s - 2}))
    pl.when(both(odd, s < last))(lambda: greet(next_chip))
    mate_count = smp_count - 1

    def gather(count):
        return lambda: pl.semaphore_wait(barrier, mate_count + count)

    pl.when(s == 0)(gather(1))
    pl.when(both(even, s > 0))(gather(2))
    pl.when(s == 1)(gather(3))
    pl.when(both(odd, both(s > 1, s < last)))(gather(4))
    pl.when(s == last)(gather(2))

    def remote(src, dst, send, recv, target):
        return pltpu.make_async_remote_copy(
            src_ref=src, dst_ref=dst, send_sem=send, recv_sem=recv,
            device_id=target, device_id_type=MESH,
        )

    def mate_copy(k, c):
        rows = pl.ds(c * piece, piece)
        return remote(
            g_hbm.at[rows], mates.at[k - 1, rows],
            mate_send.at[k - 1, c], mate_recv.at[k - 1, c],
            {"smp": lax.rem(q + k, smp_count)},
        )

    def rim_copy(k, c):
        rows = pl.ds(c * piece, piece)
        return remote(
            g_hbm.at[rows] if k == 0 else mates.at[k - 1, rows], rim.at[k, rows],
            rim_send.at[k, c], rim_recv.at[k, c], right,
        )

    def chain_copy(kind, h, src, dst, target):
        return remote(src.at[h], dst.at[h], chain_send.at[kind, h], chain_recv.at[kind, h], target)

    def x1_copy(h):
        return chain_copy(0, h, w1_out, x1_in, next_chip)

    def x1_on(h):
        return chain_copy(1, h, x1_in, x1_pass, left)

    def y_copy(h):
        return chain_copy(2, h, y_out, y_in, left)

    def h_copy(h):
        return chain_copy(3, h, h_out, h_in, right)

    def x2_copy(h):
        return chain_copy(4, h, w2_out, x2_in, next_chip)

    def x2_on(h):
        return chain_copy(5, h, x2_in, x2_pass, left)

    def v_copy(h):
        return chain_copy(6, h, v_out, v_in, right)

    u_copies = [
        remote(u_high, in_high, u_send.at[0], u_recv.at[0], right),
        remote(u_low, in_low, u_send.at[1], u_recv.at[1], right),
    ]

    for c in range(CHUNKS):
        for k in range(1, smp_count):
            mate_copy(k, c).start()

    @pl.when(s < last)
    def _():
        for c in range(CHUNKS):
            rim_copy(0, c).start()

    for copy in locals_:
        copy.wait()

    def own_grams(ref):
        a, b = ref[:, a_rows], ref[:, b_rows]
        return [gram(a, a), gram(b, b), gram(b, a)]

    def cross_grams(ref, other):
        a, b = ref[:, a_rows], ref[:, b_rows]
        return [gram(a, other[:, a_rows]), gram(a, other[:, b_rows]), gram(b, other[:, b_rows])]

    def take(c):
        for k in range(1, smp_count):
            mate_copy(k, c).wait_recv()

            @pl.when(s < last)
            def _():
                rim_copy(k, c).start()

    inverse = [halves(b_ref[0]), halves(b_ref[1])]
    own = own_grams(g_ref)
    for c in range(CHUNKS // 2):
        take(c)

    @pl.when(s > 0)
    def _():
        for c in range(CHUNKS):
            rim_copy(0, c).wait_recv()
        for n, block in enumerate(cross_grams(g_ref, rim.at[0])):
            cross[n] = block

    for c in range(CHUNKS // 2, CHUNKS):
        take(c)
    for k in range(1, smp_count):
        own = [x + y for x, y in zip(own, own_grams(mates.at[k - 1]))]
    own = [x * (1.0 / total) for x in own]
    a_aa, a_bb, a_ba = halves(own[0]), halves(own[1]), halves(own[2])
    a_ab = halves(own[2].T)
    s21 = halves(-wide(inverse[1], halves(wide(a_ba, inverse[0]))))
    v_a = wide(inverse[0], halves(m_ref[a_rows]))
    v_b = wide(inverse[1], halves(m_ref[b_rows] - wide(a_ba, halves(v_a))))

    for h in range(PARTS):
        cols = slice(h * wide_part, (h + 1) * wide_part)
        for rows, value in ((a_rows, v_a), (b_rows, v_b)):
            v_f32[h, rows] = value[:, cols]
            v_out[h, rows] = joined(value[:, cols])

    @pl.when(even)
    def _():
        for h in range(PARTS):
            v_copy(h).start()

    @pl.when(s > 0)
    def _():
        for c in range(CHUNKS):
            for k in range(1, smp_count):
                rim_copy(k, c).wait_recv()
        blocks = [cross[n] for n in range(3)]
        for k in range(1, smp_count):
            blocks = [x + y for x, y in zip(blocks, cross_grams(mates.at[k - 1], rim.at[k]))]
        row = lax.broadcasted_iota(jnp.int32, (grp, grp), 0)
        col = lax.broadcasted_iota(jnp.int32, (grp, grp), 1)
        within = col >= row
        a0, a1, b1 = [x * (1.0 / total) for x in blocks]
        a0, b1 = jnp.where(within, a0, 0.0), jnp.where(within, b1, 0.0)
        for n, block in enumerate((a0, a1, b1)):
            cross[n] = block
        a0, a1, b1 = halves(a0), halves(a1), halves(b1)

        def put(rows, cols, value):
            high, low = halves(-value)
            u_high[rows, cols] = high
            u_low[rows, cols] = low

        put(a_rows, a_rows, wide(inverse[0], a0))
        put(a_rows, b_rows, wide(inverse[0], a1))
        put(b_rows, a_rows, wide(s21, a0))
        put(b_rows, b_rows, wide(s21, a1) + wide(inverse[1], b1))

        @pl.when(even)
        def _():
            for copy in u_copies:
                copy.start()

        for n in range(3):
            high, low = halves(cross[n].T)
            c_high[n] = high
            c_low[n] = low

    def send_y(h):
        own_a, own_b = w1_out[h, a_rows], w1_out[h, b_rows]
        y_out[h, a_rows] = joined(pair_dot((c_high[0], c_low[0]), own_a))
        y_out[h, b_rows] = joined(
            pair_dot((c_high[1], c_low[1]), own_a) + pair_dot((c_high[2], c_low[2]), own_b)
        )
        y_copy(h).start()

    def u():
        return u_high[...], u_low[...]

    def chip():
        return chip_high[...], chip_low[...]

    @pl.when(odd)
    def _():
        @pl.when(s > 1)
        def _():
            for copy in u_copies:
                copy.wait_recv()
            high, low = halves(wide(u(), (in_high[...], in_low[...])))
            chip_high[...] = high
            chip_low[...] = low

        for h in range(PARTS):
            v_copy(h).wait_recv()
            v_f32[h] += pair_dot(u(), v_in[h])

    for h in range(PARTS):
        @pl.when(s < 2)
        def _():
            w1_f32[h] = v_f32[h]
            w1_out[h] = joined(v_f32[h])

        @pl.when(both(even, s > 0))
        def _():
            x1_on(h).wait_recv()
            value = v_f32[h] + pair_dot(u(), x1_pass[h])
            w1_f32[h] = value
            w1_out[h] = joined(value)

        @pl.when(both(odd, s > 1))
        def _():
            x1_copy(h).wait_recv()
            x1_on(h).start()
            value = v_f32[h] + pair_dot(chip(), x1_in[h])
            w1_f32[h] = value
            w1_out[h] = joined(value)

        @pl.when(both(odd, s < last))
        def _():
            x1_copy(h).start()

        @pl.when(both(even, s > 0))
        def _():
            send_y(h)

    @pl.when(odd)
    def _():
        for h in range(PARTS):
            send_y(h)

    for h in range(PARTS):
        cols = slice(h * wide_part, (h + 1) * wide_part)
        w1_a, w1_b = w1_f32[h, a_rows], w1_f32[h, b_rows]
        pair_a, pair_b = w1_out[h, a_rows], w1_out[h, b_rows]
        m_a, m_b = m_ref[a_rows][:, cols], m_ref[b_rows][:, cols]
        r_a = m_a - RIDGE * w1_a - pair_dot(a_aa, pair_a) - pair_dot(a_ab, pair_b)
        h_a = w1_a + pair_dot(inverse[0], joined(r_a))
        r_b = m_b - RIDGE * w1_b - pair_dot(a_bb, pair_b) - pair_dot(a_ba, joined(h_a))
        h_f32[h, a_rows] = h_a
        h_f32[h, b_rows] = w1_b + pair_dot(inverse[1], joined(r_b))

    for h in range(PARTS):
        @pl.when(s < last)
        def _():
            y_copy(h).wait_recv()
            y_a, y_b = y_in[h, a_rows], y_in[h, b_rows]
            h_f32[h, a_rows] -= pair_dot(inverse[0], y_a)
            h_f32[h, b_rows] -= pair_dot(s21, y_a) + pair_dot(inverse[1], y_b)

        @pl.when(even)
        def _():
            h_out[h] = joined(h_f32[h])
            h_copy(h).start()

    for h in range(PARTS):
        @pl.when(odd)
        def _():
            h_copy(h).wait_recv()
            h_f32[h] += pair_dot(u(), h_in[h])

    for h in range(PARTS):
        @pl.when(both(even, s > 0))
        def _():
            x2_on(h).wait_recv()
            if_even = h_f32[h] + pair_dot(u(), x2_pass[h])
            h_f32[h] = if_even

        @pl.when(both(odd, s > 1))
        def _():
            x2_copy(h).wait_recv()
            x2_on(h).start()
            h_f32[h] += pair_dot(chip(), x2_in[h])

        @pl.when(both(odd, s < last))
        def _():
            w2_out[h] = joined(h_f32[h])
            x2_copy(h).start()

    w_ref[...] = jnp.concatenate([h_f32[h] for h in range(PARTS)], 1)
    out = pltpu.make_async_copy(w_ref, w_hbm, local_sem.at[0])
    out.start()
    out.wait()

    for c in range(CHUNKS):
        for k in range(1, smp_count):
            mate_copy(k, c).wait_send()

    @pl.when(s < last)
    def _():
        for c in range(CHUNKS):
            for k in range(smp_count):
                rim_copy(k, c).wait_send()

    def sent(*copies):
        def wait():
            for copy in copies:
                for h in range(PARTS):
                    copy(h).wait_send()
        return wait

    pl.when(s > 0)(sent(y_copy))
    pl.when(even)(sent(v_copy, h_copy))
    pl.when(both(odd, s < last))(sent(x1_copy, x2_copy))
    pl.when(both(odd, s > 1))(sent(x1_on, x2_on))

    @pl.when(both(even, s > 0))
    def _():
        for copy in u_copies:
            copy.wait_send()


def solution(mesh):
    var_count, smp_count = mesh.shape["var"], mesh.shape["smp"]

    def per_device(genotypes, marginal, block_inverse):
        samples, variants = genotypes.shape
        traits = marginal.shape[1]
        grp = block_inverse.shape[1]
        part_f32 = pltpu.VMEM((PARTS, variants, traits // PARTS), F32)
        pair = pltpu.VMEM((PARTS, variants, 2 * traits // PARTS), BF16)
        square = pltpu.VMEM((variants, variants), BF16)
        mates = max(1, smp_count - 1)
        dma = pltpu.SemaphoreType.DMA
        return pl.pallas_call(
            functools.partial(kernel, var_count, smp_count, samples * smp_count),
            out_shape=jax.ShapeDtypeStruct(marginal.shape, F32),
            in_specs=[pl.BlockSpec(memory_space=pltpu.HBM)] * 3,
            out_specs=pl.BlockSpec(memory_space=pltpu.HBM),
            scratch_shapes=[
                pltpu.VMEM((samples, variants), BF16),
                pltpu.VMEM((variants, traits), F32),
                pltpu.VMEM(block_inverse.shape, F32),
                pltpu.VMEM((variants, traits), F32),
                pltpu.VMEM((mates, samples, variants), BF16),
                pltpu.VMEM((smp_count, samples, variants), BF16),
                pltpu.VMEM((3, grp, grp), F32),
            ]
            + [square] * 6
            + [pltpu.VMEM((3, grp, grp), BF16)] * 2
            + [part_f32, pair, pair, part_f32, part_f32]
            + [pair] * 10
            + [
                dma((3,)),
                dma((mates, CHUNKS)),
                dma((mates, CHUNKS)),
                dma((smp_count, CHUNKS)),
                dma((smp_count, CHUNKS)),
                dma((2,)),
                dma((2,)),
                dma((7, PARTS)),
                dma((7, PARTS)),
            ],
            compiler_params=pltpu.CompilerParams(
                collective_id=0, has_side_effects=True, vmem_limit_bytes=48 * 1024 * 1024
            ),
        )(genotypes, marginal, block_inverse)

    return jax.shard_map(
        per_device,
        mesh=mesh,
        in_specs=(P("smp", "var"), P("var", "smp"), P("var", None, None)),
        out_specs=P("var", "smp"),
        check_vma=False,
    )
```

```python
import functools

import jax
import jax.numpy as jnp
from jax import lax
from jax.experimental import pallas as pl
from jax.experimental.pallas import tpu as pltpu
from jax.sharding import PartitionSpec as P

RIDGE = 0.5
CHUNKS = 4
PARTS = 2
MESH = pl.DeviceIdType.MESH
F32 = jnp.float32
BF16 = jnp.bfloat16


def halves(x):
    high = x.astype(BF16)
    low = (x - high.astype(F32)).astype(BF16)
    return high, low


def dot(a, b):
    return jnp.dot(a, b, preferred_element_type=F32)


def gram(a, b):
    return lax.dot_general(a, b, (((0,), (0,)), ((), ())), preferred_element_type=F32)


def wide(a, b):
    return dot(a[0], b[0]) + (dot(a[0], b[1]) + dot(a[1], b[0]))


def pair_dot(a, both):
    n = both.shape[1] // 2
    first = dot(a[0], both)
    return first[:, :n] + (first[:, n:] + dot(a[1], both[:, :n]))


def joined(x):
    return jnp.concatenate(halves(x), 1)


def kernel(
    var_count, smp_count, total,
    g_hbm, m_hbm, b_hbm, w_ref,
    g_ref, m_ref, b_ref,
    mates, rim, cross, u_high, u_low, in_high, in_low, chip_high, chip_low,
    map_high, map_low, far_high, far_low, c_high, c_low,
    v_f32, v_out, v_in, w1_f32, h_f32, w1_out, x1_in, x1_pass, y_out, y_in, h_out, h_in,
    w2_out, x2_in, x2_pass, c0_out, c0_in, far_out, far_in,
    local_sem, mate_send, mate_recv, rim_send, rim_recv, u_send, u_recv, chain_send, chain_recv,
):
    s = lax.axis_index("var")
    q = lax.axis_index("smp")
    last = var_count - 1
    grp = b_ref.shape[1]
    samples = g_ref.shape[0]
    piece = samples // CHUNKS
    wide_part = m_ref.shape[1] // PARTS
    even = lax.rem(s, 2) == 0
    odd = jnp.logical_not(even)
    right, left = {"var": s + 1}, {"var": s - 1}
    next_chip = {"var": s + 2}
    a_rows, b_rows = pl.ds(0, grp), pl.ds(grp, grp)
    both = jnp.logical_and

    locals_ = [
        pltpu.make_async_copy(g_hbm, g_ref, local_sem.at[0]),
        pltpu.make_async_copy(m_hbm, m_ref, local_sem.at[1]),
        pltpu.make_async_copy(b_hbm, b_ref, local_sem.at[2]),
    ]
    for copy in locals_:
        copy.start()

    barrier = pltpu.get_barrier_semaphore()

    def greet(target):
        pl.semaphore_signal(barrier, inc=1, device_id=target, device_id_type=MESH)

    for k in range(1, smp_count):
        greet({"smp": lax.rem(q + k, smp_count)})
    pl.when(s > 0)(lambda: greet(left))
    pl.when(s < last)(lambda: greet(right))
    pl.when(both(odd, s > 1))(lambda: greet({"var": s - 2}))
    pl.when(both(odd, s < last))(lambda: greet(next_chip))
    mate_count = smp_count - 1

    def gather(count):
        return lambda: pl.semaphore_wait(barrier, mate_count + count)

    pl.when(s == 0)(gather(1))
    pl.when(both(even, s > 0))(gather(2))
    pl.when(s == 1)(gather(3))
    pl.when(both(odd, both(s > 1, s < last)))(gather(4))
    pl.when(s == last)(gather(2))

    def remote(src, dst, send, recv, target):
        return pltpu.make_async_remote_copy(
            src_ref=src, dst_ref=dst, send_sem=send, recv_sem=recv,
            device_id=target, device_id_type=MESH,
        )

    def mate_copy(k, c):
        rows = pl.ds(c * piece, piece)
        return remote(
            g_hbm.at[rows], mates.at[k - 1, rows],
            mate_send.at[k - 1, c], mate_recv.at[k - 1, c],
            {"smp": lax.rem(q + k, smp_count)},
        )

    def rim_copy(k, c):
        rows = pl.ds(c * piece, piece)
        return remote(
            g_hbm.at[rows] if k == 0 else mates.at[k - 1, rows], rim.at[k, rows],
            rim_send.at[k, c], rim_recv.at[k, c], right,
        )

    def chain_copy(kind, h, src, dst, target):
        return remote(src.at[h], dst.at[h], chain_send.at[kind, h], chain_recv.at[kind, h], target)

    def x1_copy(h):
        return chain_copy(0, h, w1_out, x1_in, next_chip)

    def x1_on(h):
        return chain_copy(1, h, x1_in, x1_pass, left)

    def y_copy(h):
        return chain_copy(2, h, y_out, y_in, left)

    def h_copy(h):
        return chain_copy(3, h, h_out, h_in, right)

    def x2_copy(h):
        return chain_copy(4, h, w2_out, x2_in, next_chip)

    def x2_on(h):
        return chain_copy(5, h, x2_in, x2_pass, left)

    def v_copy(h):
        return chain_copy(6, h, v_out, v_in, right)

    u_copies = [
        remote(u_high, in_high, u_send.at[0], u_recv.at[0], right),
        remote(u_low, in_low, u_send.at[1], u_recv.at[1], right),
    ]

    def c0_copy(h):
        return chain_copy(7, h, c0_out, c0_in, right)

    def far_copy(h):
        return chain_copy(8, h, far_out, far_in, {"var": s - 2})

    map_copies = [
        remote(map_high, far_high, u_send.at[2], u_recv.at[2], right),
        remote(map_low, far_low, u_send.at[3], u_recv.at[3], right),
    ]

    for c in range(CHUNKS):
        for k in range(1, smp_count):
            mate_copy(k, c).start()

    @pl.when(s < last)
    def _():
        for c in range(CHUNKS):
            rim_copy(0, c).start()

    for copy in locals_:
        copy.wait()

    def own_grams(ref):
        a, b = ref[:, a_rows], ref[:, b_rows]
        return [gram(a, a), gram(b, b), gram(b, a)]

    def cross_grams(ref, other):
        a, b = ref[:, a_rows], ref[:, b_rows]
        return [gram(a, other[:, a_rows]), gram(a, other[:, b_rows]), gram(b, other[:, b_rows])]

    def take(c):
        for k in range(1, smp_count):
            mate_copy(k, c).wait_recv()

            @pl.when(s < last)
            def _():
                rim_copy(k, c).start()

    inverse = [halves(b_ref[0]), halves(b_ref[1])]
    own = own_grams(g_ref)
    for c in range(CHUNKS // 2):
        take(c)

    @pl.when(s > 0)
    def _():
        for c in range(CHUNKS):
            rim_copy(0, c).wait_recv()
        for n, block in enumerate(cross_grams(g_ref, rim.at[0])):
            cross[n] = block

    for c in range(CHUNKS // 2, CHUNKS):
        take(c)
    for k in range(1, smp_count):
        own = [x + y for x, y in zip(own, own_grams(mates.at[k - 1]))]
    own = [x * (1.0 / total) for x in own]
    a_aa, a_bb, a_ba = halves(own[0]), halves(own[1]), halves(own[2])
    a_ab = halves(own[2].T)
    s21 = halves(-wide(inverse[1], halves(wide(a_ba, inverse[0]))))
    v_a = wide(inverse[0], halves(m_ref[a_rows]))
    v_b = wide(inverse[1], halves(m_ref[b_rows] - wide(a_ba, halves(v_a))))

    for h in range(PARTS):
        cols = slice(h * wide_part, (h + 1) * wide_part)
        for rows, value in ((a_rows, v_a), (b_rows, v_b)):
            v_f32[h, rows] = value[:, cols]
            v_out[h, rows] = joined(value[:, cols])

    @pl.when(even)
    def _():
        for h in range(PARTS):
            v_copy(h).start()

    def couple(ref, h, out):
        own_a, own_b = ref[h, a_rows], ref[h, b_rows]
        out[h, a_rows] = joined(pair_dot((c_high[0], c_low[0]), own_a))
        out[h, b_rows] = joined(
            pair_dot((c_high[1], c_low[1]), own_a) + pair_dot((c_high[2], c_low[2]), own_b)
        )

    @pl.when(s > 0)
    def _():
        for c in range(CHUNKS):
            for k in range(1, smp_count):
                rim_copy(k, c).wait_recv()
        blocks = [cross[n] for n in range(3)]
        for k in range(1, smp_count):
            blocks = [x + y for x, y in zip(blocks, cross_grams(mates.at[k - 1], rim.at[k]))]
        row = lax.broadcasted_iota(jnp.int32, (grp, grp), 0)
        col = lax.broadcasted_iota(jnp.int32, (grp, grp), 1)
        within = col >= row
        a0, a1, b1 = [x * (1.0 / total) for x in blocks]
        a0, b1 = jnp.where(within, a0, 0.0), jnp.where(within, b1, 0.0)
        for n, block in enumerate((a0, a1, b1)):
            cross[n] = block
        a0, a1, b1 = halves(a0), halves(a1), halves(b1)

        def put(rows, cols, value):
            high, low = halves(-value)
            u_high[rows, cols] = high
            u_low[rows, cols] = low

        put(a_rows, a_rows, wide(inverse[0], a0))
        put(a_rows, b_rows, wide(inverse[0], a1))
        put(b_rows, a_rows, wide(s21, a0))
        put(b_rows, b_rows, wide(s21, a1) + wide(inverse[1], b1))

        @pl.when(even)
        def _():
            for copy in u_copies:
                copy.start()

        for n in range(3):
            high, low = halves(cross[n].T)
            c_high[n] = high
            c_low[n] = low

        @pl.when(even)
        def _():
            top = u_high[a_rows], u_low[a_rows]
            low_rows = u_high[b_rows], u_low[b_rows]
            c = [(c_high[n], c_low[n]) for n in range(3)]
            high, low = halves(wide(c[0], top))
            map_high[a_rows] = high
            map_low[a_rows] = low
            high, low = halves(wide(c[1], top) + wide(c[2], low_rows))
            map_high[b_rows] = high
            map_low[b_rows] = low
            for copy in map_copies:
                copy.start()
            for h in range(PARTS):
                couple(v_out, h, c0_out)
                c0_copy(h).start()

    def u():
        return u_high[...], u_low[...]

    def chip():
        return chip_high[...], chip_low[...]

    @pl.when(odd)
    def _():
        for h in range(PARTS):
            v_copy(h).wait_recv()
            v_f32[h] += pair_dot(u(), v_in[h])

        @pl.when(s > 1)
        def _():
            for copy in u_copies:
                copy.wait_recv()
            high, low = halves(wide(u(), (in_high[...], in_low[...])))
            chip_high[...] = high
            chip_low[...] = low
            for copy in map_copies:
                copy.wait_recv()
            for h in range(PARTS):
                c0_copy(h).wait_recv()

    for h in range(PARTS):
        @pl.when(s < 2)
        def _():
            w1_f32[h] = v_f32[h]
            w1_out[h] = joined(v_f32[h])

        @pl.when(both(even, s > 0))
        def _():
            x1_on(h).wait_recv()
            value = v_f32[h] + pair_dot(u(), x1_pass[h])
            w1_f32[h] = value
            w1_out[h] = joined(value)

        @pl.when(both(odd, s > 1))
        def _():
            x1_copy(h).wait_recv()
            x1_on(h).start()
            value = v_f32[h] + pair_dot(chip(), x1_in[h])
            w1_f32[h] = value
            w1_out[h] = joined(value)

        @pl.when(both(odd, s < last))
        def _():
            x1_copy(h).start()

        @pl.when(both(odd, s > 1))
        def _():
            sent_by = (c0_in[h].astype(F32), far_high[...], far_low[...])
            start = sent_by[0][:, :wide_part] + sent_by[0][:, wide_part:]
            far_out[h] = joined(start + pair_dot(sent_by[1:], x1_in[h]))
            far_copy(h).start()

    @pl.when(odd)
    def _():
        for h in range(PARTS):
            couple(w1_out, h, y_out)
            y_copy(h).start()

    for h in range(PARTS):
        cols = slice(h * wide_part, (h + 1) * wide_part)
        w1_a, w1_b = w1_f32[h, a_rows], w1_f32[h, b_rows]
        pair_a, pair_b = w1_out[h, a_rows], w1_out[h, b_rows]
        m_a, m_b = m_ref[a_rows][:, cols], m_ref[b_rows][:, cols]
        r_a = m_a - RIDGE * w1_a - pair_dot(a_aa, pair_a) - pair_dot(a_ab, pair_b)
        h_a = w1_a + pair_dot(inverse[0], joined(r_a))
        r_b = m_b - RIDGE * w1_b - pair_dot(a_bb, pair_b) - pair_dot(a_ba, joined(h_a))
        h_f32[h, a_rows] = h_a
        h_f32[h, b_rows] = w1_b + pair_dot(inverse[1], joined(r_b))

    def couple_back(h, ref):
        y_a, y_b = ref[h, a_rows], ref[h, b_rows]
        h_f32[h, a_rows] -= pair_dot(inverse[0], y_a)
        h_f32[h, b_rows] -= pair_dot(s21, y_a) + pair_dot(inverse[1], y_b)

    for h in range(PARTS):
        @pl.when(both(odd, s < last))
        def _():
            far_copy(h).wait_recv()
            couple_back(h, far_in)

        @pl.when(even)
        def _():
            y_copy(h).wait_recv()
            couple_back(h, y_in)

        @pl.when(even)
        def _():
            h_out[h] = joined(h_f32[h])
            h_copy(h).start()

    for h in range(PARTS):
        @pl.when(odd)
        def _():
            h_copy(h).wait_recv()
            h_f32[h] += pair_dot(u(), h_in[h])

    for h in range(PARTS):
        @pl.when(both(even, s > 0))
        def _():
            x2_on(h).wait_recv()
            if_even = h_f32[h] + pair_dot(u(), x2_pass[h])
            h_f32[h] = if_even

        @pl.when(both(odd, s > 1))
        def _():
            x2_copy(h).wait_recv()
            x2_on(h).start()
            h_f32[h] += pair_dot(chip(), x2_in[h])

        @pl.when(both(odd, s < last))
        def _():
            w2_out[h] = joined(h_f32[h])
            x2_copy(h).start()

    w_ref[...] = jnp.concatenate([h_f32[h] for h in range(PARTS)], 1)
    for c in range(CHUNKS):
        for k in range(1, smp_count):
            mate_copy(k, c).wait_send()

    @pl.when(s < last)
    def _():
        for c in range(CHUNKS):
            for k in range(smp_count):
                rim_copy(k, c).wait_send()

    def sent(*copies):
        def wait():
            for copy in copies:
                for h in range(PARTS):
                    copy(h).wait_send()
        return wait

    pl.when(odd)(sent(y_copy))
    pl.when(even)(sent(v_copy, h_copy))
    pl.when(both(odd, s < last))(sent(x1_copy, x2_copy))
    pl.when(both(odd, s > 1))(sent(x1_on, x2_on, far_copy))
    pl.when(both(even, s > 0))(sent(c0_copy))

    @pl.when(both(even, s > 0))
    def _():
        for copy in u_copies + map_copies:
            copy.wait_send()


def solution(mesh):
    var_count, smp_count = mesh.shape["var"], mesh.shape["smp"]

    def per_device(genotypes, marginal, block_inverse):
        samples, variants = genotypes.shape
        traits = marginal.shape[1]
        grp = block_inverse.shape[1]
        part_f32 = pltpu.VMEM((PARTS, variants, traits // PARTS), F32)
        pair = pltpu.VMEM((PARTS, variants, 2 * traits // PARTS), BF16)
        square = pltpu.VMEM((variants, variants), BF16)
        mates = max(1, smp_count - 1)
        dma = pltpu.SemaphoreType.DMA
        return pl.pallas_call(
            functools.partial(kernel, var_count, smp_count, samples * smp_count),
            out_shape=jax.ShapeDtypeStruct(marginal.shape, F32),
            in_specs=[pl.BlockSpec(memory_space=pltpu.HBM)] * 3,
            out_specs=pl.BlockSpec(memory_space=pltpu.VMEM),
            scratch_shapes=[
                pltpu.VMEM((samples, variants), BF16),
                pltpu.VMEM((variants, traits), F32),
                pltpu.VMEM(block_inverse.shape, F32),
                pltpu.VMEM((mates, samples, variants), BF16),
                pltpu.VMEM((smp_count, samples, variants), BF16),
                pltpu.VMEM((3, grp, grp), F32),
            ]
            + [square] * 10
            + [pltpu.VMEM((3, grp, grp), BF16)] * 2
            + [part_f32, pair, pair, part_f32, part_f32]
            + [pair] * 14
            + [
                dma((3,)),
                dma((mates, CHUNKS)),
                dma((mates, CHUNKS)),
                dma((smp_count, CHUNKS)),
                dma((smp_count, CHUNKS)),
                dma((4,)),
                dma((4,)),
                dma((9, PARTS)),
                dma((9, PARTS)),
            ],
            compiler_params=pltpu.CompilerParams(
                collective_id=0, has_side_effects=True, vmem_limit_bytes=(64 * 1024 - 96) * 1024
            ),
        )(genotypes, marginal, block_inverse)

    return jax.shard_map(
        per_device,
        mesh=mesh,
        in_specs=(P("smp", "var"), P("var", "smp"), P("var", None, None)),
        out_specs=P("var", "smp"),
        check_vma=False,
    )
```

```python
import functools

import jax
import jax.numpy as jnp
from jax import lax
from jax.experimental import pallas as pl
from jax.experimental.pallas import tpu as pltpu
from jax.sharding import PartitionSpec as P

RIDGE = 0.5
CHUNKS = 4
PARTS = 2
MESH = pl.DeviceIdType.MESH
F32 = jnp.float32
BF16 = jnp.bfloat16


def halves(x):
    high = x.astype(BF16)
    low = (x - high.astype(F32)).astype(BF16)
    return high, low


def dot(a, b):
    return jnp.dot(a, b, preferred_element_type=F32)


def gram(a, b):
    return lax.dot_general(a, b, (((0,), (0,)), ((), ())), preferred_element_type=F32)


def wide(a, b):
    return dot(a[0], b[0]) + (dot(a[0], b[1]) + dot(a[1], b[0]))


def pair_dot(a, both):
    n = both.shape[1] // 2
    first = dot(a[0], both)
    return first[:, :n] + (first[:, n:] + dot(a[1], both[:, :n]))


def joined(x):
    return jnp.concatenate(halves(x), 1)


def kernel(
    var_count, smp_count, total,
    g_hbm, m_hbm, b_hbm, w_ref,
    g_ref, m_ref, b_ref,
    mates, rim, cross, u_high, u_low, in_high, in_low, chip_high, chip_low,
    map_high, map_low, far_high, far_low, c_high, c_low,
    v_f32, v_out, v_in, w1_f32, h_f32, w1_out, x1_in, x1_pass, y_out, y_in, h_out, h_in,
    w2_out, x2_in, x2_pass, c0_out, c0_in, far_out, far_in,
    local_sem, mate_send, mate_recv, rim_send, rim_recv, u_send, u_recv, chain_send, chain_recv,
):
    s = lax.axis_index("var")
    q = lax.axis_index("smp")
    last = var_count - 1
    grp = b_ref.shape[1]
    samples = g_ref.shape[0]
    piece = samples // CHUNKS
    wide_part = m_ref.shape[1] // PARTS
    even = lax.rem(s, 2) == 0
    odd = jnp.logical_not(even)
    right, left = {"var": s + 1}, {"var": s - 1}
    next_chip = {"var": s + 2}
    a_rows, b_rows = pl.ds(0, grp), pl.ds(grp, grp)
    both = jnp.logical_and

    locals_ = [
        pltpu.make_async_copy(g_hbm, g_ref, local_sem.at[0]),
        pltpu.make_async_copy(m_hbm, m_ref, local_sem.at[1]),
        pltpu.make_async_copy(b_hbm, b_ref, local_sem.at[2]),
    ]
    for copy in locals_:
        copy.start()

    barrier = pltpu.get_barrier_semaphore()

    def greet(target):
        pl.semaphore_signal(barrier, inc=1, device_id=target, device_id_type=MESH)

    for k in range(1, smp_count):
        greet({"smp": lax.rem(q + k, smp_count)})
    pl.when(s > 0)(lambda: greet(left))
    pl.when(s < last)(lambda: greet(right))
    pl.when(both(odd, s > 1))(lambda: greet({"var": s - 2}))
    pl.when(both(odd, s < last))(lambda: greet(next_chip))
    mate_count = smp_count - 1

    def gather(count):
        return lambda: pl.semaphore_wait(barrier, mate_count + count)

    pl.when(s == 0)(gather(1))
    pl.when(both(even, s > 0))(gather(2))
    pl.when(s == 1)(gather(3))
    pl.when(both(odd, both(s > 1, s < last)))(gather(4))
    pl.when(s == last)(gather(2))

    def remote(src, dst, send, recv, target):
        return pltpu.make_async_remote_copy(
            src_ref=src, dst_ref=dst, send_sem=send, recv_sem=recv,
            device_id=target, device_id_type=MESH,
        )

    def mate_copy(k, c):
        rows = pl.ds(c * piece, piece)
        return remote(
            g_hbm.at[rows], mates.at[k - 1, rows],
            mate_send.at[k - 1, c], mate_recv.at[k - 1, c],
            {"smp": lax.rem(q + k, smp_count)},
        )

    def rim_copy(k, c):
        rows = pl.ds(c * piece, piece)
        return remote(
            g_hbm.at[rows] if k == 0 else mates.at[k - 1, rows], rim.at[k, rows],
            rim_send.at[k, c], rim_recv.at[k, c], right,
        )

    def chain_copy(kind, h, src, dst, target):
        return remote(src.at[h], dst.at[h], chain_send.at[kind, h], chain_recv.at[kind, h], target)

    def x1_copy(h):
        return chain_copy(0, h, w1_out, x1_in, next_chip)

    def x1_on(h):
        return chain_copy(1, h, x1_in, x1_pass, left)

    def y_copy(h):
        return chain_copy(2, h, y_out, y_in, left)

    def h_copy(h):
        return chain_copy(3, h, h_out, h_in, right)

    def x2_copy(h):
        return chain_copy(4, h, w2_out, x2_in, next_chip)

    def x2_on(h):
        return chain_copy(5, h, x2_in, x2_pass, left)

    def v_copy(h):
        return chain_copy(6, h, v_out, v_in, right)

    u_copies = [
        remote(u_high, in_high, u_send.at[0], u_recv.at[0], right),
        remote(u_low, in_low, u_send.at[1], u_recv.at[1], right),
    ]

    def c0_copy(h):
        return chain_copy(7, h, c0_out, c0_in, right)

    def far_copy(h):
        return chain_copy(8, h, far_out, far_in, {"var": s - 2})

    map_copies = [
        remote(map_high, far_high, u_send.at[2], u_recv.at[2], right),
        remote(map_low, far_low, u_send.at[3], u_recv.at[3], right),
    ]

    for c in range(CHUNKS):
        for k in range(1, smp_count):
            mate_copy(k, c).start()

    @pl.when(s < last)
    def _():
        for c in range(CHUNKS):
            rim_copy(0, c).start()

    for copy in locals_:
        copy.wait()

    def own_grams(ref):
        a, b = ref[:, a_rows], ref[:, b_rows]
        return [gram(a, a), gram(b, b), gram(b, a)]

    def cross_grams(ref, other):
        a, b = ref[:, a_rows], ref[:, b_rows]
        return [gram(a, other[:, a_rows]), gram(a, other[:, b_rows]), gram(b, other[:, b_rows])]

    def take(c):
        for k in range(1, smp_count):
            mate_copy(k, c).wait_recv()

            @pl.when(s < last)
            def _():
                rim_copy(k, c).start()

    inverse = [halves(b_ref[0]), halves(b_ref[1])]
    own = own_grams(g_ref)
    for c in range(CHUNKS // 2):
        take(c)

    @pl.when(s > 0)
    def _():
        for c in range(CHUNKS):
            rim_copy(0, c).wait_recv()
        for n, block in enumerate(cross_grams(g_ref, rim.at[0])):
            cross[n] = block

    for c in range(CHUNKS // 2, CHUNKS):
        take(c)
    for k in range(1, smp_count):
        own = [x + y for x, y in zip(own, own_grams(mates.at[k - 1]))]
    own = [x * (1.0 / total) for x in own]
    a_aa, a_bb, a_ba = halves(own[0]), halves(own[1]), halves(own[2])
    a_ab = halves(own[2].T)
    s21 = halves(-wide(inverse[1], halves(wide(a_ba, inverse[0]))))
    v_a = wide(inverse[0], halves(m_ref[a_rows]))
    v_b = wide(inverse[1], halves(m_ref[b_rows] - wide(a_ba, halves(v_a))))

    for h in range(PARTS):
        cols = slice(h * wide_part, (h + 1) * wide_part)
        for rows, value in ((a_rows, v_a), (b_rows, v_b)):
            v_f32[h, rows] = value[:, cols]
            v_out[h, rows] = joined(value[:, cols])

    @pl.when(even)
    def _():
        for h in range(PARTS):
            v_copy(h).start()

    def couple(ref, h, out):
        own_a, own_b = ref[h, a_rows], ref[h, b_rows]
        out[h, a_rows] = joined(pair_dot((c_high[0], c_low[0]), own_a))
        out[h, b_rows] = joined(
            pair_dot((c_high[1], c_low[1]), own_a) + pair_dot((c_high[2], c_low[2]), own_b)
        )

    @pl.when(s > 0)
    def _():
        for c in range(CHUNKS):
            for k in range(1, smp_count):
                rim_copy(k, c).wait_recv()
        blocks = [cross[n] for n in range(3)]
        for k in range(1, smp_count):
            blocks = [x + y for x, y in zip(blocks, cross_grams(mates.at[k - 1], rim.at[k]))]
        row = lax.broadcasted_iota(jnp.int32, (grp, grp), 0)
        col = lax.broadcasted_iota(jnp.int32, (grp, grp), 1)
        within = col >= row
        a0, a1, b1 = [x * (1.0 / total) for x in blocks]
        a0, b1 = jnp.where(within, a0, 0.0), jnp.where(within, b1, 0.0)
        for n, block in enumerate((a0, a1, b1)):
            cross[n] = block
        a0, a1, b1 = halves(a0), halves(a1), halves(b1)

        def put(rows, cols, value):
            high, low = halves(-value)
            u_high[rows, cols] = high
            u_low[rows, cols] = low

        put(a_rows, a_rows, wide(inverse[0], a0))
        put(a_rows, b_rows, wide(inverse[0], a1))
        put(b_rows, a_rows, wide(s21, a0))
        put(b_rows, b_rows, wide(s21, a1) + wide(inverse[1], b1))

        @pl.when(even)
        def _():
            for copy in u_copies:
                copy.start()

        for n in range(3):
            high, low = halves(cross[n].T)
            c_high[n] = high
            c_low[n] = low

        @pl.when(even)
        def _():
            for h in range(PARTS):
                couple(v_out, h, c0_out)
                c0_copy(h).start()
            top = u_high[a_rows], u_low[a_rows]
            low_rows = u_high[b_rows], u_low[b_rows]
            c = [(c_high[n], c_low[n]) for n in range(3)]
            high, low = halves(wide(c[0], top))
            map_high[a_rows] = high
            map_low[a_rows] = low
            high, low = halves(wide(c[1], top) + wide(c[2], low_rows))
            map_high[b_rows] = high
            map_low[b_rows] = low
            for copy in map_copies:
                copy.start()

    def u():
        return u_high[...], u_low[...]

    def chip():
        return chip_high[...], chip_low[...]

    @pl.when(odd)
    def _():
        for h in range(PARTS):
            v_copy(h).wait_recv()
            v_f32[h] += pair_dot(u(), v_in[h])

        @pl.when(s > 1)
        def _():
            for copy in u_copies:
                copy.wait_recv()
            high, low = halves(wide(u(), (in_high[...], in_low[...])))
            chip_high[...] = high
            chip_low[...] = low

    for h in range(PARTS):
        @pl.when(s < 2)
        def _():
            w1_f32[h] = v_f32[h]
            w1_out[h] = joined(v_f32[h])

        @pl.when(both(even, s > 0))
        def _():
            x1_on(h).wait_recv()
            value = v_f32[h] + pair_dot(u(), x1_pass[h])
            w1_f32[h] = value
            w1_out[h] = joined(value)

        @pl.when(both(odd, s > 1))
        def _():
            x1_copy(h).wait_recv()
            x1_on(h).start()
            value = v_f32[h] + pair_dot(chip(), x1_in[h])
            w1_f32[h] = value
            w1_out[h] = joined(value)

        @pl.when(both(odd, s < last))
        def _():
            x1_copy(h).start()

        @pl.when(both(odd, s > 1))
        def _():
            if h == 0:
                for copy in map_copies:
                    copy.wait_recv()
            c0_copy(h).wait_recv()
            sent_by = (c0_in[h].astype(F32), far_high[...], far_low[...])
            start = sent_by[0][:, :wide_part] + sent_by[0][:, wide_part:]
            far_out[h] = joined(start + pair_dot(sent_by[1:], x1_in[h]))
            far_copy(h).start()

    @pl.when(odd)
    def _():
        for h in range(PARTS):
            couple(w1_out, h, y_out)
            y_copy(h).start()

    for h in range(PARTS):
        cols = slice(h * wide_part, (h + 1) * wide_part)
        w1_a, w1_b = w1_f32[h, a_rows], w1_f32[h, b_rows]
        pair_a, pair_b = w1_out[h, a_rows], w1_out[h, b_rows]
        m_a, m_b = m_ref[a_rows][:, cols], m_ref[b_rows][:, cols]
        r_a = m_a - RIDGE * w1_a - pair_dot(a_aa, pair_a) - pair_dot(a_ab, pair_b)
        h_a = w1_a + pair_dot(inverse[0], joined(r_a))
        r_b = m_b - RIDGE * w1_b - pair_dot(a_bb, pair_b) - pair_dot(a_ba, joined(h_a))
        h_f32[h, a_rows] = h_a
        h_f32[h, b_rows] = w1_b + pair_dot(inverse[1], joined(r_b))

    def couple_back(h, ref):
        y_a, y_b = ref[h, a_rows], ref[h, b_rows]
        h_f32[h, a_rows] -= pair_dot(inverse[0], y_a)
        h_f32[h, b_rows] -= pair_dot(s21, y_a) + pair_dot(inverse[1], y_b)

    for h in range(PARTS):
        @pl.when(even)
        def _():
            y_copy(h).wait_recv()
            couple_back(h, y_in)
            h_out[h] = joined(h_f32[h])
            h_copy(h).start()

    for h in range(PARTS):
        @pl.when(odd)
        def _():
            h_copy(h).wait_recv()
            h_f32[h] += pair_dot(u(), h_in[h])

    for h in range(PARTS):
        @pl.when(both(odd, s < last))
        def _():
            far_copy(h).wait_recv()
            couple_back(h, far_in)

        @pl.when(both(even, s > 0))
        def _():
            x2_on(h).wait_recv()
            if_even = h_f32[h] + pair_dot(u(), x2_pass[h])
            h_f32[h] = if_even

        @pl.when(both(odd, s > 1))
        def _():
            x2_copy(h).wait_recv()
            x2_on(h).start()
            h_f32[h] += pair_dot(chip(), x2_in[h])

        @pl.when(both(odd, s < last))
        def _():
            w2_out[h] = joined(h_f32[h])
            x2_copy(h).start()

    w_ref[...] = jnp.concatenate([h_f32[h] for h in range(PARTS)], 1)
    for c in range(CHUNKS):
        for k in range(1, smp_count):
            mate_copy(k, c).wait_send()

    @pl.when(s < last)
    def _():
        for c in range(CHUNKS):
            for k in range(smp_count):
                rim_copy(k, c).wait_send()

    def sent(*copies):
        def wait():
            for copy in copies:
                for h in range(PARTS):
                    copy(h).wait_send()
        return wait

    pl.when(odd)(sent(y_copy))
    pl.when(even)(sent(v_copy, h_copy))
    pl.when(both(odd, s < last))(sent(x1_copy, x2_copy))
    pl.when(both(odd, s > 1))(sent(x1_on, x2_on, far_copy))
    pl.when(both(even, s > 0))(sent(c0_copy))

    @pl.when(both(even, s > 0))
    def _():
        for copy in u_copies + map_copies:
            copy.wait_send()


def solution(mesh):
    var_count, smp_count = mesh.shape["var"], mesh.shape["smp"]

    def per_device(genotypes, marginal, block_inverse):
        samples, variants = genotypes.shape
        traits = marginal.shape[1]
        grp = block_inverse.shape[1]
        part_f32 = pltpu.VMEM((PARTS, variants, traits // PARTS), F32)
        pair = pltpu.VMEM((PARTS, variants, 2 * traits // PARTS), BF16)
        square = pltpu.VMEM((variants, variants), BF16)
        mates = max(1, smp_count - 1)
        dma = pltpu.SemaphoreType.DMA
        return pl.pallas_call(
            functools.partial(kernel, var_count, smp_count, samples * smp_count),
            out_shape=jax.ShapeDtypeStruct(marginal.shape, F32),
            in_specs=[pl.BlockSpec(memory_space=pltpu.HBM)] * 3,
            out_specs=pl.BlockSpec(memory_space=pltpu.VMEM),
            scratch_shapes=[
                pltpu.VMEM((samples, variants), BF16),
                pltpu.VMEM((variants, traits), F32),
                pltpu.VMEM(block_inverse.shape, F32),
                pltpu.VMEM((mates, samples, variants), BF16),
                pltpu.VMEM((smp_count, samples, variants), BF16),
                pltpu.VMEM((3, grp, grp), F32),
            ]
            + [square] * 10
            + [pltpu.VMEM((3, grp, grp), BF16)] * 2
            + [part_f32, pair, pair, part_f32, part_f32]
            + [pair] * 14
            + [
                dma((3,)),
                dma((mates, CHUNKS)),
                dma((mates, CHUNKS)),
                dma((smp_count, CHUNKS)),
                dma((smp_count, CHUNKS)),
                dma((4,)),
                dma((4,)),
                dma((9, PARTS)),
                dma((9, PARTS)),
            ],
            compiler_params=pltpu.CompilerParams(
                collective_id=0, has_side_effects=True, vmem_limit_bytes=(64 * 1024 - 96) * 1024
            ),
        )(genotypes, marginal, block_inverse)

    return jax.shard_map(
        per_device,
        mesh=mesh,
        in_specs=(P("smp", "var"), P("var", "smp"), P("var", None, None)),
        out_specs=P("var", "smp"),
        check_vma=False,
    )
```

```python
import functools

import jax
import jax.numpy as jnp
from jax import lax
from jax.experimental import pallas as pl
from jax.experimental.pallas import tpu as pltpu
from jax.sharding import PartitionSpec as P

RIDGE = 0.5
CHUNKS = 8
PARTS = 2
MESH = pl.DeviceIdType.MESH
F32 = jnp.float32
BF16 = jnp.bfloat16


def halves(x):
    high = x.astype(BF16)
    low = (x - high.astype(F32)).astype(BF16)
    return high, low


def dot(a, b):
    return jnp.dot(a, b, preferred_element_type=F32)


def gram(a, b):
    return lax.dot_general(a, b, (((0,), (0,)), ((), ())), preferred_element_type=F32)


def wide(a, b):
    return dot(a[0], b[0]) + (dot(a[0], b[1]) + dot(a[1], b[0]))


def pair_dot(a, both):
    n = both.shape[1] // 2
    first = dot(a[0], both)
    return first[:, :n] + (first[:, n:] + dot(a[1], both[:, :n]))


def joined(x):
    return jnp.concatenate(halves(x), 1)


def kernel(
    var_count, smp_count, total,
    g_hbm, m_hbm, b_hbm, w_ref,
    g_ref, m_ref, b_ref,
    mates, rim, cross, u_high, u_low, in_high, in_low, chip_high, chip_low,
    map_high, map_low, far_high, far_low, c_high, c_low,
    v_f32, v_out, v_in, w1_f32, h_f32, w1_out, x1_in, x1_pass, y_out, y_in, h_out, h_in,
    w2_out, x2_in, x2_pass, c0_out, c0_in, far_out, far_in,
    local_sem, mate_send, mate_recv, rim_send, rim_recv, u_send, u_recv, chain_send, chain_recv,
):
    s = lax.axis_index("var")
    q = lax.axis_index("smp")
    last = var_count - 1
    grp = b_ref.shape[1]
    samples = g_ref.shape[0]
    piece = samples // CHUNKS
    wide_part = m_ref.shape[1] // PARTS
    even = lax.rem(s, 2) == 0
    odd = jnp.logical_not(even)
    right, left = {"var": s + 1}, {"var": s - 1}
    next_chip = {"var": s + 2}
    a_rows, b_rows = pl.ds(0, grp), pl.ds(grp, grp)
    both = jnp.logical_and

    locals_ = [
        pltpu.make_async_copy(g_hbm, g_ref, local_sem.at[0]),
        pltpu.make_async_copy(m_hbm, m_ref, local_sem.at[1]),
        pltpu.make_async_copy(b_hbm, b_ref, local_sem.at[2]),
    ]
    for copy in locals_:
        copy.start()

    barrier = pltpu.get_barrier_semaphore()

    def greet(target):
        pl.semaphore_signal(barrier, inc=1, device_id=target, device_id_type=MESH)

    for k in range(1, smp_count):
        greet({"smp": lax.rem(q + k, smp_count)})
    pl.when(s > 0)(lambda: greet(left))
    pl.when(s < last)(lambda: greet(right))
    pl.when(both(odd, s > 1))(lambda: greet({"var": s - 2}))
    pl.when(both(odd, s < last))(lambda: greet(next_chip))
    mate_count = smp_count - 1

    def gather(count):
        return lambda: pl.semaphore_wait(barrier, mate_count + count)

    pl.when(s == 0)(gather(1))
    pl.when(both(even, s > 0))(gather(2))
    pl.when(s == 1)(gather(3))
    pl.when(both(odd, both(s > 1, s < last)))(gather(4))
    pl.when(s == last)(gather(2))

    def remote(src, dst, send, recv, target):
        return pltpu.make_async_remote_copy(
            src_ref=src, dst_ref=dst, send_sem=send, recv_sem=recv,
            device_id=target, device_id_type=MESH,
        )

    def mate_copy(k, c):
        rows = pl.ds(c * piece, piece)
        return remote(
            g_hbm.at[rows], mates.at[k - 1, rows],
            mate_send.at[k - 1, c], mate_recv.at[k - 1, c],
            {"smp": lax.rem(q + k, smp_count)},
        )

    def rim_copy(k, c):
        rows = pl.ds(c * piece, piece)
        return remote(
            g_hbm.at[rows] if k == 0 else mates.at[k - 1, rows], rim.at[k, rows],
            rim_send.at[k, c], rim_recv.at[k, c], right,
        )

    def chain_copy(kind, h, src, dst, target):
        return remote(src.at[h], dst.at[h], chain_send.at[kind, h], chain_recv.at[kind, h], target)

    def x1_copy(h):
        return chain_copy(0, h, w1_out, x1_in, next_chip)

    def x1_on(h):
        return chain_copy(1, h, x1_in, x1_pass, left)

    def y_copy(h):
        return chain_copy(2, h, y_out, y_in, left)

    def h_copy(h):
        return chain_copy(3, h, h_out, h_in, right)

    def x2_copy(h):
        return chain_copy(4, h, w2_out, x2_in, next_chip)

    def x2_on(h):
        return chain_copy(5, h, x2_in, x2_pass, left)

    def v_copy(h):
        return chain_copy(6, h, v_out, v_in, right)

    u_copies = [
        remote(u_high, in_high, u_send.at[0], u_recv.at[0], right),
        remote(u_low, in_low, u_send.at[1], u_recv.at[1], right),
    ]

    def c0_copy(h):
        return chain_copy(7, h, c0_out, c0_in, right)

    def far_copy(h):
        return chain_copy(8, h, far_out, far_in, {"var": s - 2})

    map_copies = [
        remote(map_high, far_high, u_send.at[2], u_recv.at[2], right),
        remote(map_low, far_low, u_send.at[3], u_recv.at[3], right),
    ]

    for c in range(CHUNKS):
        for k in range(1, smp_count):
            mate_copy(k, c).start()

    @pl.when(s < last)
    def _():
        for c in range(CHUNKS):
            rim_copy(0, c).start()

    for copy in locals_:
        copy.wait()

    def own_grams(ref):
        a, b = ref[:, a_rows], ref[:, b_rows]
        return [gram(a, a), gram(b, b), gram(b, a)]

    def cross_grams(ref, other):
        a, b = ref[:, a_rows], ref[:, b_rows]
        return [gram(a, other[:, a_rows]), gram(a, other[:, b_rows]), gram(b, other[:, b_rows])]

    def take(c):
        for k in range(1, smp_count):
            mate_copy(k, c).wait_recv()

            @pl.when(s < last)
            def _():
                rim_copy(k, c).start()

    inverse = [halves(b_ref[0]), halves(b_ref[1])]
    own = own_grams(g_ref)
    for c in range(CHUNKS // 2):
        take(c)

    @pl.when(s > 0)
    def _():
        for c in range(CHUNKS):
            rim_copy(0, c).wait_recv()
        for n, block in enumerate(cross_grams(g_ref, rim.at[0])):
            cross[n] = block

    for c in range(CHUNKS // 2, CHUNKS):
        take(c)
    for k in range(1, smp_count):
        own = [x + y for x, y in zip(own, own_grams(mates.at[k - 1]))]
    own = [x * (1.0 / total) for x in own]
    a_aa, a_bb, a_ba = halves(own[0]), halves(own[1]), halves(own[2])
    a_ab = halves(own[2].T)
    s21 = halves(-wide(inverse[1], halves(wide(a_ba, inverse[0]))))
    v_a = wide(inverse[0], halves(m_ref[a_rows]))
    v_b = wide(inverse[1], halves(m_ref[b_rows] - wide(a_ba, halves(v_a))))

    for h in range(PARTS):
        cols = slice(h * wide_part, (h + 1) * wide_part)
        for rows, value in ((a_rows, v_a), (b_rows, v_b)):
            v_f32[h, rows] = value[:, cols]
            v_out[h, rows] = joined(value[:, cols])

    @pl.when(even)
    def _():
        for h in range(PARTS):
            v_copy(h).start()

    def couple(ref, h, out):
        own_a, own_b = ref[h, a_rows], ref[h, b_rows]
        out[h, a_rows] = joined(pair_dot((c_high[0], c_low[0]), own_a))
        out[h, b_rows] = joined(
            pair_dot((c_high[1], c_low[1]), own_a) + pair_dot((c_high[2], c_low[2]), own_b)
        )

    @pl.when(s > 0)
    def _():
        for c in range(CHUNKS):
            for k in range(1, smp_count):
                rim_copy(k, c).wait_recv()
        blocks = [cross[n] for n in range(3)]
        for k in range(1, smp_count):
            blocks = [x + y for x, y in zip(blocks, cross_grams(mates.at[k - 1], rim.at[k]))]
        row = lax.broadcasted_iota(jnp.int32, (grp, grp), 0)
        col = lax.broadcasted_iota(jnp.int32, (grp, grp), 1)
        within = col >= row
        a0, a1, b1 = [x * (1.0 / total) for x in blocks]
        a0, b1 = jnp.where(within, a0, 0.0), jnp.where(within, b1, 0.0)
        for n, block in enumerate((a0, a1, b1)):
            cross[n] = block
        a0, a1, b1 = halves(a0), halves(a1), halves(b1)

        def put(rows, cols, value):
            high, low = halves(-value)
            u_high[rows, cols] = high
            u_low[rows, cols] = low

        put(a_rows, a_rows, wide(inverse[0], a0))
        put(a_rows, b_rows, wide(inverse[0], a1))
        put(b_rows, a_rows, wide(s21, a0))
        put(b_rows, b_rows, wide(s21, a1) + wide(inverse[1], b1))

        @pl.when(even)
        def _():
            for copy in u_copies:
                copy.start()

        for n in range(3):
            high, low = halves(cross[n].T)
            c_high[n] = high
            c_low[n] = low

        @pl.when(even)
        def _():
            for h in range(PARTS):
                couple(v_out, h, c0_out)
                c0_copy(h).start()
            top = u_high[a_rows], u_low[a_rows]
            low_rows = u_high[b_rows], u_low[b_rows]
            c = [(c_high[n], c_low[n]) for n in range(3)]
            high, low = halves(wide(c[0], top))
            map_high[a_rows] = high
            map_low[a_rows] = low
            high, low = halves(wide(c[1], top) + wide(c[2], low_rows))
            map_high[b_rows] = high
            map_low[b_rows] = low
            for copy in map_copies:
                copy.start()

    def u():
        return u_high[...], u_low[...]

    def chip():
        return chip_high[...], chip_low[...]

    @pl.when(odd)
    def _():
        for h in range(PARTS):
            v_copy(h).wait_recv()
            v_f32[h] += pair_dot(u(), v_in[h])

        @pl.when(s > 1)
        def _():
            for copy in u_copies:
                copy.wait_recv()
            high, low = halves(wide(u(), (in_high[...], in_low[...])))
            chip_high[...] = high
            chip_low[...] = low

    for h in range(PARTS):
        @pl.when(s < 2)
        def _():
            w1_f32[h] = v_f32[h]
            w1_out[h] = joined(v_f32[h])

        @pl.when(both(even, s > 0))
        def _():
            x1_on(h).wait_recv()
            value = v_f32[h] + pair_dot(u(), x1_pass[h])
            w1_f32[h] = value
            w1_out[h] = joined(value)

        @pl.when(both(odd, s > 1))
        def _():
            x1_copy(h).wait_recv()
            x1_on(h).start()
            value = v_f32[h] + pair_dot(chip(), x1_in[h])
            w1_f32[h] = value
            w1_out[h] = joined(value)

        @pl.when(both(odd, s < last))
        def _():
            x1_copy(h).start()

        @pl.when(both(odd, s > 1))
        def _():
            if h == 0:
                for copy in map_copies:
                    copy.wait_recv()
            c0_copy(h).wait_recv()
            sent_by = (c0_in[h].astype(F32), far_high[...], far_low[...])
            start = sent_by[0][:, :wide_part] + sent_by[0][:, wide_part:]
            far_out[h] = joined(start + pair_dot(sent_by[1:], x1_in[h]))
            far_copy(h).start()

    @pl.when(odd)
    def _():
        for h in range(PARTS):
            couple(w1_out, h, y_out)
            y_copy(h).start()

    for h in range(PARTS):
        cols = slice(h * wide_part, (h + 1) * wide_part)
        w1_a, w1_b = w1_f32[h, a_rows], w1_f32[h, b_rows]
        pair_a, pair_b = w1_out[h, a_rows], w1_out[h, b_rows]
        m_a, m_b = m_ref[a_rows][:, cols], m_ref[b_rows][:, cols]
        r_a = m_a - RIDGE * w1_a - pair_dot(a_aa, pair_a) - pair_dot(a_ab, pair_b)
        h_a = w1_a + pair_dot(inverse[0], joined(r_a))
        r_b = m_b - RIDGE * w1_b - pair_dot(a_bb, pair_b) - pair_dot(a_ba, joined(h_a))
        h_f32[h, a_rows] = h_a
        h_f32[h, b_rows] = w1_b + pair_dot(inverse[1], joined(r_b))

    def couple_back(h, ref):
        y_a, y_b = ref[h, a_rows], ref[h, b_rows]
        h_f32[h, a_rows] -= pair_dot(inverse[0], y_a)
        h_f32[h, b_rows] -= pair_dot(s21, y_a) + pair_dot(inverse[1], y_b)

    for h in range(PARTS):
        @pl.when(even)
        def _():
            y_copy(h).wait_recv()
            couple_back(h, y_in)
            h_out[h] = joined(h_f32[h])
            h_copy(h).start()

    for h in range(PARTS):
        @pl.when(odd)
        def _():
            h_copy(h).wait_recv()
            h_f32[h] += pair_dot(u(), h_in[h])

    for h in range(PARTS):
        @pl.when(both(odd, s < last))
        def _():
            far_copy(h).wait_recv()
            couple_back(h, far_in)

        @pl.when(both(even, s > 0))
        def _():
            x2_on(h).wait_recv()
            if_even = h_f32[h] + pair_dot(u(), x2_pass[h])
            h_f32[h] = if_even

        @pl.when(both(odd, s > 1))
        def _():
            x2_copy(h).wait_recv()
            x2_on(h).start()
            h_f32[h] += pair_dot(chip(), x2_in[h])

        @pl.when(both(odd, s < last))
        def _():
            w2_out[h] = joined(h_f32[h])
            x2_copy(h).start()

    w_ref[...] = jnp.concatenate([h_f32[h] for h in range(PARTS)], 1)
    for c in range(CHUNKS):
        for k in range(1, smp_count):
            mate_copy(k, c).wait_send()

    @pl.when(s < last)
    def _():
        for c in range(CHUNKS):
            for k in range(smp_count):
                rim_copy(k, c).wait_send()

    def sent(*copies):
        def wait():
            for copy in copies:
                for h in range(PARTS):
                    copy(h).wait_send()
        return wait

    pl.when(odd)(sent(y_copy))
    pl.when(even)(sent(v_copy, h_copy))
    pl.when(both(odd, s < last))(sent(x1_copy, x2_copy))
    pl.when(both(odd, s > 1))(sent(x1_on, x2_on, far_copy))
    pl.when(both(even, s > 0))(sent(c0_copy))

    @pl.when(both(even, s > 0))
    def _():
        for copy in u_copies + map_copies:
            copy.wait_send()


def solution(mesh):
    var_count, smp_count = mesh.shape["var"], mesh.shape["smp"]

    def per_device(genotypes, marginal, block_inverse):
        samples, variants = genotypes.shape
        traits = marginal.shape[1]
        grp = block_inverse.shape[1]
        part_f32 = pltpu.VMEM((PARTS, variants, traits // PARTS), F32)
        pair = pltpu.VMEM((PARTS, variants, 2 * traits // PARTS), BF16)
        square = pltpu.VMEM((variants, variants), BF16)
        mates = max(1, smp_count - 1)
        dma = pltpu.SemaphoreType.DMA
        return pl.pallas_call(
            functools.partial(kernel, var_count, smp_count, samples * smp_count),
            out_shape=jax.ShapeDtypeStruct(marginal.shape, F32),
            in_specs=[pl.BlockSpec(memory_space=pltpu.HBM)] * 3,
            out_specs=pl.BlockSpec(memory_space=pltpu.VMEM),
            scratch_shapes=[
                pltpu.VMEM((samples, variants), BF16),
                pltpu.VMEM((variants, traits), F32),
                pltpu.VMEM(block_inverse.shape, F32),
                pltpu.VMEM((mates, samples, variants), BF16),
                pltpu.VMEM((smp_count, samples, variants), BF16),
                pltpu.VMEM((3, grp, grp), F32),
            ]
            + [square] * 10
            + [pltpu.VMEM((3, grp, grp), BF16)] * 2
            + [part_f32, pair, pair, part_f32, part_f32]
            + [pair] * 14
            + [
                dma((3,)),
                dma((mates, CHUNKS)),
                dma((mates, CHUNKS)),
                dma((smp_count, CHUNKS)),
                dma((smp_count, CHUNKS)),
                dma((4,)),
                dma((4,)),
                dma((9, PARTS)),
                dma((9, PARTS)),
            ],
            compiler_params=pltpu.CompilerParams(
                collective_id=0, has_side_effects=True, vmem_limit_bytes=(64 * 1024 - 96) * 1024
            ),
        )(genotypes, marginal, block_inverse)

    return jax.shard_map(
        per_device,
        mesh=mesh,
        in_specs=(P("smp", "var"), P("var", "smp"), P("var", None, None)),
        out_specs=P("var", "smp"),
        check_vma=False,
    )
```
